32 devices in a mesh: expert: 8 (over z, x), hidden: 4 (over y, core).
Axes of the slice: x: 2, y: 2, z: 4, core: 2. Of those that a mesh axis runs over, the one named last changes fastest.
Arguments:
- tokens: bfloat16 [128, 7168], P('expert', 'hidden'), may hold values from -6 to 6
- routes: int32 [128, 8], P('expert'), may hold values from 0 to 15, as said below
- combine: float32 [128, 8], P('expert'), may hold values from 0.05 to 0.5
- w_gate: bfloat16 [16, 7168, 1024], P('expert', None, 'hidden'), may hold values from -0.0625 to 0.0625
- w_up: bfloat16 [16, 7168, 1024], P('expert', None, 'hidden'), may hold values from -0.0625 to 0.0625
- w_down: bfloat16 [16, 1024, 7168], P('expert', 'hidden'), may hold values from -0.1875 to 0.1875
- cotangent: bfloat16 [128, 7168], P('expert', 'hidden'), may hold values from -6 to 6
Outputs:
- output: bfloat16 [128, 7168], P('expert', 'hidden')
- grad_tokens: bfloat16 [128, 7168], P('expert', 'hidden')
The draws below stay inside these ranges and needn't reach their ends.
Inputs may be any that keep to these rules, and one draw needn't show every extreme that they name: `routes`: each row names 8 different experts. In each aligned block of 16 rows (the rows of one device) no expert is named by more than 16 rows, and the same expert is named by exactly 16 rows in every block.
All inputs are finite; a program needn't handle non-finite values.
Results may differ from the reference program's by a relative error of at most 0.012.
Values may be sent and summed in bfloat16 or wider, within the bound.
A program may use at most 128 MiB of HBM per device.

```python
import math
import jax
import jax.numpy as jnp
from jax import lax

D = 7168
FF = 1024
TOP = 8
TOK_DEV = 16
EXPERTS = 16
TOKENS = 128
CAP = 16
N_EXPERT = 8
N_HIDDEN = 4


def draw_routes(key, part):
    blocks = TOKENS // TOK_DEV
    mean_load = TOK_DEV * TOP // EXPERTS
    pair_count = TOK_DEV * TOP
    half_count = (EXPERTS - 2) // 2
    hot_key, block_key = jax.random.split(jax.random.fold_in(key, 17))
    hot_expert = jax.random.randint(hot_key, (), 0, EXPERTS).astype(jnp.int32)
    positions = jnp.arange(pair_count, dtype=jnp.int32)

    def one_block(sub_key):
        order_key, shift_key, token_key = jax.random.split(sub_key, 3)
        others = jax.random.permutation(order_key, EXPERTS - 1).astype(jnp.int32)
        others = jnp.where(others >= hot_expert, others + 1, others)
        shifts = jax.random.randint(shift_key, (half_count,), 0, mean_load + 1).astype(jnp.int32)
        head_loads = jnp.array([2 * mean_load, 0], jnp.int32)
        loads = jnp.concatenate([head_loads, mean_load + shifts, mean_load - shifts])
        owners = jnp.concatenate([hot_expert[None], others])
        ends = jnp.cumsum(loads)
        run_index = jnp.sum((positions[:, None] >= ends[None, :]).astype(jnp.int32), axis=1)
        picks = owners[run_index].reshape(TOP, TOK_DEV).T
        return picks[jax.random.permutation(token_key, TOK_DEV)]
    block_keys = jax.random.split(block_key, blocks)
    return jax.vmap(one_block)(block_keys).reshape(TOKENS, TOP).astype(jnp.int32)


def block_levels(rng, extent, cuts, smallest, high):
    def one(dim, parts):
        draws = jax.random.uniform(jax.random.fold_in(jax.random.fold_in(rng, 6), dim), (parts,), jnp.float32, smallest / len(cuts), high / len(cuts))
        return jnp.repeat(jnp.exp(draws), extent[dim] // parts).reshape((-1,) + (1,) * (len(extent) - dim - 1))

    loudness = one(*cuts[0])
    for cut in cuts[1:]:
        loudness = loudness * one(*cut)
    return loudness


def normal_values(stream_key, shape, spread, limit, cuts=(), kind=jnp.bfloat16):
    drawn = jax.random.normal(stream_key, shape, jnp.float32) * spread
    if len(cuts) > 0:
        drawn = block_levels(stream_key, shape, cuts, -0.22, 0.18) * drawn
    return jnp.clip(drawn, min=-limit, max=limit).astype(kind)


def setup_inputs(seed: int = 0) -> dict:
    seeds = jax.random.split(jax.random.key(seed), 8)
    tokens = normal_values(seeds[0], (TOKENS, D), 1.0, 6.0, ((0, 8), (1, 4)))
    routes = draw_routes(jax.random.fold_in(seeds[7], 71), 0)
    combine = jnp.clip(jnp.exp(math.log(0.5) - 2.3025851 * jax.random.uniform(seeds[2], (TOKENS, TOP), jnp.float32) ** block_levels(seeds[2], (TOKENS, TOP), ((0, 8),), -0.2, 0.2)), 0.05, 0.5)
    w_gate = normal_values(seeds[3], (EXPERTS, D, FF), D ** -0.5, 0.0625, ((0, 8), (2, 4)))
    w_up = normal_values(seeds[4], (EXPERTS, D, FF), D ** -0.5, 0.0625, ((0, 8), (2, 4)))
    w_down = normal_values(seeds[5], (EXPERTS, FF, D), FF ** -0.5, 0.1875, ((0, 8), (1, 4)))
    cotangent = normal_values(seeds[6], (TOKENS, D), 1.0, 6.0, ((0, 8), (1, 4)))
    return {"tokens": tokens, "routes": routes, "combine": combine, "w_gate": w_gate, "w_up": w_up, "w_down": w_down, "cotangent": cotangent}


def expert_pass(rows_in, grads_in, gate_weight, up_weight, down_weight):
    gate_pre = jnp.dot(rows_in, gate_weight, preferred_element_type=jnp.float32)
    up_pre = jnp.dot(rows_in, up_weight, preferred_element_type=jnp.float32)
    sigmoid_gate = jax.nn.sigmoid(gate_pre)
    activated = gate_pre * sigmoid_gate
    hidden_act = (activated * up_pre).astype(jnp.bfloat16)
    back_hidden = jnp.dot(grads_in, down_weight.T, preferred_element_type=jnp.float32)
    grad_gate = (back_hidden * up_pre * sigmoid_gate * (1.0 + gate_pre * (1.0 - sigmoid_gate))).astype(jnp.bfloat16)
    grad_up = (back_hidden * activated).astype(jnp.bfloat16)
    quarter_units = FF // N_HIDDEN
    out_total = jnp.zeros((rows_in.shape[0], D), jnp.float32)
    grad_total = jnp.zeros((rows_in.shape[0], D), jnp.float32)
    for quarter in range(N_HIDDEN):
        lower = quarter * quarter_units
        upper = lower + quarter_units
        out_part = jnp.dot(hidden_act[:, lower:upper], down_weight[lower:upper], preferred_element_type=jnp.float32)
        out_part = lax.optimization_barrier(out_part.astype(jnp.bfloat16))
        out_total = out_total + out_part.astype(jnp.float32)
        grad_part = jnp.dot(grad_gate[:, lower:upper], gate_weight[:, lower:upper].T, preferred_element_type=jnp.float32)
        grad_part = grad_part + jnp.dot(grad_up[:, lower:upper], up_weight[:, lower:upper].T, preferred_element_type=jnp.float32)
        grad_part = lax.optimization_barrier(grad_part.astype(jnp.bfloat16))
        grad_total = grad_total + grad_part.astype(jnp.float32)
    return out_total.astype(jnp.bfloat16), grad_total.astype(jnp.bfloat16)


def reference(tokens, routes, combine, w_gate, w_up, w_down, cotangent):
    pair_count = TOKENS * TOP
    flat_routes = routes.reshape(pair_count).astype(jnp.int32)
    order = jnp.argsort(flat_routes, stable=True).astype(jnp.int32)
    expert_ids = jnp.arange(EXPERTS, dtype=jnp.int32)
    counts = jnp.sum((flat_routes[None, :] == expert_ids[:, None]).astype(jnp.int32), axis=1).astype(jnp.int32)
    starts = (jnp.cumsum(counts) - counts).astype(jnp.int32)
    buffer_rows = N_EXPERT * CAP
    padded_order = jnp.concatenate([order, jnp.zeros((buffer_rows,), jnp.int32)])
    flat_combine = combine.reshape(pair_count)

    def per_expert(totals, expert):
        out_total, grad_total = totals
        chosen = lax.dynamic_slice_in_dim(padded_order, starts[expert], buffer_rows)
        live = jnp.arange(buffer_rows, dtype=jnp.int32) < counts[expert]
        token_index = (chosen // TOP).astype(jnp.int32)
        scale = jnp.where(live, flat_combine[chosen], jnp.zeros((buffer_rows,), jnp.float32))
        out_rows, grad_rows = expert_pass(tokens[token_index], cotangent[token_index], w_gate[expert], w_up[expert], w_down[expert])
        out_total = out_total.at[token_index].add(scale[:, None] * out_rows.astype(jnp.float32))
        grad_total = grad_total.at[token_index].add(scale[:, None] * grad_rows.astype(jnp.float32))
        return (out_total, grad_total), None

    zero_total = jnp.zeros((TOKENS, D), jnp.float32)
    (out_total, grad_total), _ = lax.scan(per_expert, (zero_total, zero_total), expert_ids)
    return out_total.astype(jnp.bfloat16), grad_total.astype(jnp.bfloat16)
```

```python
import jax
import jax.numpy as jnp
from jax import lax
from jax.experimental import pallas as pl
from jax.experimental.pallas import tpu as pltpu
from jax.sharding import PartitionSpec as P


def per_device(tokens, routes, combine, w_gate, w_up, w_down, cotangent):
    tok_rows = tokens.shape[0]
    top_count = routes.shape[1]
    local_experts = w_gate.shape[0]
    sources = lax.axis_size("expert")
    experts = local_experts * sources
    pair_count = tok_rows * top_count
    capacity = 2 * pair_count // experts
    flat_routes = routes.reshape(pair_count)
    onehot = (flat_routes[:, None] == jnp.arange(experts, dtype=jnp.int32)[None, :]).astype(
        jnp.int32
    )
    slot_rank = jnp.sum((jnp.cumsum(onehot, axis=0) - 1) * onehot, axis=1)
    target = flat_routes * capacity + slot_rank
    slot_table = (
        jnp.full((experts * capacity,), pair_count, jnp.int32)
        .at[target]
        .set(jnp.arange(pair_count, dtype=jnp.int32))
    )
    source_rows = slot_table // top_count

    def pack_rows(values):
        padded = jnp.concatenate([values, jnp.zeros((1, values.shape[1]), values.dtype)], axis=0)
        return padded[source_rows].reshape(experts, capacity, values.shape[1])

    def to_local(arrived):
        columns = arrived.shape[2]
        sectioned = arrived.reshape(sources, local_experts, capacity, columns).transpose(1, 0, 2, 3)
        return sectioned.reshape(local_experts, sources * capacity, columns)

    def to_global(leaving):
        columns = leaving.shape[2]
        sectioned = leaving.reshape(local_experts, sources, capacity, columns).transpose(1, 0, 2, 3)
        return sectioned.reshape(experts, capacity, columns)

    def unpack(returned):
        flattened = returned.reshape(experts * capacity, returned.shape[2])
        picked = (
            flattened[target].astype(jnp.float32).reshape(tok_rows, top_count, returned.shape[2])
        )
        return jnp.sum(picked * combine[:, :, None], axis=1).astype(jnp.bfloat16)

    full_tokens, full_grads = (
        lax.all_gather(tokens, "hidden", axis=1, tiled=True),
        lax.all_gather(cotangent, "hidden", axis=1, tiled=True),
    )
    arrived_x, arrived_dy = (
        lax.all_to_all(pack_rows(full_tokens), "expert", split_axis=0, concat_axis=0, tiled=True),
        lax.all_to_all(pack_rows(full_grads), "expert", split_axis=0, concat_axis=0, tiled=True),
    )
    arrived_x = to_local(arrived_x)
    arrived_dy = to_local(arrived_dy)
    gate_pre = jnp.einsum("erd,edf->erf", arrived_x, w_gate, preferred_element_type=jnp.float32)
    up_pre = jnp.einsum("erd,edf->erf", arrived_x, w_up, preferred_element_type=jnp.float32)
    back_hidden = jnp.einsum("erd,efd->erf", arrived_dy, w_down, preferred_element_type=jnp.float32)
    sigmoid_gate = jax.nn.sigmoid(gate_pre)
    activated = gate_pre * sigmoid_gate
    hidden_act = (activated * up_pre).astype(jnp.bfloat16)
    out_terms = jnp.einsum(
        "erf,efd->erd", hidden_act, w_down, preferred_element_type=jnp.float32
    ).astype(jnp.bfloat16)
    grad_gate = (
        back_hidden * up_pre * sigmoid_gate * (1.0 + gate_pre * (1.0 - sigmoid_gate))
    ).astype(jnp.bfloat16)
    grad_up = (back_hidden * activated).astype(jnp.bfloat16)
    out_share = (
        lax.psum_scatter(out_terms, "hidden", scatter_dimension=2, tiled=True)
        .astype(jnp.float32)
        .astype(jnp.bfloat16)
    )
    out_back = lax.all_to_all(
        to_global(out_share), "expert", split_axis=0, concat_axis=0, tiled=True
    )
    grad_terms = jnp.einsum("erf,edf->erd", grad_gate, w_gate, preferred_element_type=jnp.float32)
    grad_terms = grad_terms + jnp.einsum(
        "erf,edf->erd", grad_up, w_up, preferred_element_type=jnp.float32
    )
    grad_share = lax.psum_scatter(
        grad_terms.astype(jnp.bfloat16), "hidden", scatter_dimension=2, tiled=True
    )
    grad_back = lax.all_to_all(
        to_global(grad_share), "expert", split_axis=0, concat_axis=0, tiled=True
    )
    return (unpack(out_back), unpack(grad_back))


SPECS = (
    P("expert", "hidden"),
    P("expert", None),
    P("expert", None),
    P("expert", None, "hidden"),
    P("expert", None, "hidden"),
    P("expert", "hidden", None),
    P("expert", "hidden"),
)
MESH = pl.DeviceIdType.MESH
ROWS = 16
ORDER = (1, 3, 2)
F32 = jnp.float32
BF16 = jnp.bfloat16
GT, GC, GW, RO, RG = 0, 31, 62, 66, 83
COPIES = 100


def dot_nt(a, b):
    return lax.dot_general(a, b, (((1,), (1,)), ((), ())), preferred_element_type=F32)


def kernel(
    tok, cot, routes, comb, wg_hbm, wu_hbm, wd_hbm, out, grad,
    X, Y, wg, wu, wd, cb, gacc, uacc, bacc, H, G,
    PO, PG, RcO, RcG, RyO, RxO, RzO, RxG, RyG, RzG, ssem, rsem, lsem,
):
    e, h = lax.axis_index("expert"), lax.axis_index("hidden")
    z, x, y, c = e // 2, e % 2, h // 2, h % 2
    xn, yn, cn = 1 - x, 1 - y, 1 - c
    cols = tok.shape[1]
    units = wd_hbm.shape[1]
    dev_x, dev_y, dev_s = (z * 2 + xn, h), (e, yn * 2 + c), (e, y * 2 + cn)
    dev_z = {i: (((z + i) % 4) * 2 + x, h) for i in ORDER}

    def rows(xx, zz):
        return pl.ds(pl.multiple_of((xx * 4 + zz) * ROWS, ROWS), ROWS)

    def half(zz):
        return pl.ds(pl.multiple_of(zz * ROWS, ROWS), ROWS)

    started = []

    def send(src, dst, k, dev):
        copy = pltpu.make_async_remote_copy(
            src_ref=src, dst_ref=dst, send_sem=ssem.at[k], recv_sem=rsem.at[k],
            device_id=dev, device_id_type=MESH,
        )
        copy.start()
        started.append(copy)

    def arrive(ref, k, dev):
        pltpu.make_async_remote_copy(
            src_ref=ref, dst_ref=ref, send_sem=ssem.at[k], recv_sem=rsem.at[k],
            device_id=dev, device_id_type=MESH,
        ).wait_recv()

    barrier = pltpu.get_barrier_semaphore()
    partners = [dev_x, dev_y, dev_s] + [dev_z[i] for i in ORDER]
    for dev in partners:
        pl.semaphore_signal(barrier, inc=1, device_id=dev, device_id_type=MESH)

    X[h, rows(x, z), :] = tok[...]
    Y[h, rows(x, z), :] = cot[...]
    lane = lax.broadcasted_iota(jnp.int32, (ROWS, 128), 1)
    expert = jnp.where(lane < 16, lane, lane - 16)
    dense = jnp.zeros((ROWS, 128), F32)
    for k in range(routes.shape[1]):
        dense = dense + jnp.where(expert == routes[:, k : k + 1], comb[:, k : k + 1], 0.0)
    high = dense.astype(BF16)
    low = (dense - high.astype(F32)).astype(BF16)
    cb[rows(x, z), :] = jnp.where(lane < 16, high.astype(F32), low.astype(F32)).astype(BF16)
    pl.semaphore_wait(barrier, len(partners))

    def near(i):
        return (z - i) % 4

    def blk(buf, yy, cc, xx, zz):
        return buf.at[yy * 2 + cc, rows(xx, zz), :]

    def first(arr, i):
        buf, base, dev1, dev2 = arr
        ref = blk(buf, y, c, x, near(i))
        send(ref, ref, base + 3 + i, dev1)
        send(ref, ref, base + 7 + i, dev2)

    def sib(arr, yo, xo, i):
        ref = blk(arr[0], (y, yn)[yo], c, (x, xn)[xo], near(i))
        send(ref, ref, arr[1] + 15 + 8 * yo + 4 * xo + i, dev_s)

    def sib_arrive(arr, yo, xo, i):
        ref = blk(arr[0], (y, yn)[yo], cn, (x, xn)[xo], near(i))
        arrive(ref, arr[1] + 15 + 8 * yo + 4 * xo + i, dev_s)

    TOKS, COTS = (X, GT, dev_x, dev_y), (Y, GC, dev_y, dev_x)
    BOTH = (TOKS, COTS)
    for i in ORDER:
        for arr in BOTH:
            ref = blk(arr[0], y, c, x, z)
            send(ref, ref, arr[1] + i - 1, dev_z[i])
        if i == ORDER[0]:
            for arr in BOTH:
                first(arr, 0)
    for i in ORDER:
        ref = cb.at[rows(x, z), :]
        send(ref, ref, GW + i - 1, dev_z[i])
    for arr in BOTH:
        sib(arr, 0, 0, 0)

    wcopies = [
        pltpu.make_async_copy(wg_hbm, wg, lsem.at[0]),
        pltpu.make_async_copy(wu_hbm, wu, lsem.at[1]),
    ]
    for hh in range(4):
        for j in range(2):
            wcopies.append(
                pltpu.make_async_copy(
                    wd_hbm.at[j, :, pl.ds(hh * cols, cols)],
                    wd.at[hh, pl.ds(j * units, units), :],
                    lsem.at[2 + hh * 2 + j],
                )
            )
    for copy in wcopies:
        copy.start()

    for i in ORDER:
        for arr in BOTH:
            arrive(blk(arr[0], y, c, x, near(i)), arr[1] + i - 1, dev_z[i])
            first(arr, i)
            sib(arr, 0, 0, i)
    for i in ORDER:
        arrive(cb.at[rows(x, near(i)), :], GW + i - 1, dev_z[i])
    mine = cb.at[pl.ds(pl.multiple_of(x * 64, 64), 64), :]
    send(mine, mine, GW + 3, dev_x)
    for i in (0,) + ORDER:
        ref = blk(X, y, c, xn, near(i))
        arrive(ref, GT + 3 + i, dev_x)
        send(ref, ref, GT + 11 + i, dev_y)
        sib(TOKS, 0, 1, i)
        ref = blk(Y, yn, c, x, near(i))
        arrive(ref, GC + 3 + i, dev_y)
        send(ref, ref, GC + 11 + i, dev_x)
        sib(COTS, 1, 0, i)

    gacc[...] = jnp.zeros_like(gacc)
    uacc[...] = jnp.zeros_like(uacc)
    bacc[...] = jnp.zeros_like(bacc)

    def project(hh):
        at = pl.ds(pl.multiple_of(hh * cols, cols), cols)
        for j in range(2):
            own = slice(j * units, (j + 1) * units)
            gacc[:, own] += jnp.dot(X[hh], wg[j, at, :], preferred_element_type=F32)
            uacc[:, own] += jnp.dot(X[hh], wu[j, at, :], preferred_element_type=F32)

    wcopies[0].wait()
    wcopies[1].wait()
    for xo in range(2):
        for i in range(4):
            sib_arrive(TOKS, 0, xo, i)
    lax.fori_loop(0, 2, lambda k, _: (project(y * 2 + k), 0)[1], 0)

    for a in range(2):
        for i in (0,) + ORDER:
            arrive(blk(X, yn, c, (x, xn)[a], near(i)), GT + 7 + 4 * a + i, dev_y)
            sib(TOKS, 1, a, i)
            arrive(blk(Y, (y, yn)[a], c, xn, near(i)), GC + 7 + 4 * a + i, dev_x)
            sib(COTS, a, 1, i)
    for xo in range(2):
        for i in range(4):
            sib_arrive(TOKS, 1, xo, i)
    lax.fori_loop(0, 2, lambda k, _: (project(yn * 2 + k), 0)[1], 0)
    for copy in wcopies[2:]:
        copy.wait()
    for yo in range(2):
        for xo in range(2):
            for i in range(4):
                sib_arrive(COTS, yo, xo, i)

    def back(hh, _):
        bacc[...] += dot_nt(Y[hh], wd[hh])
        return 0

    lax.fori_loop(0, 4, back, 0)
    other = cb.at[pl.ds(pl.multiple_of(xn * 64, 64), 64), :]
    arrive(other, GW + 3, dev_x)
    wide = lax.broadcasted_iota(jnp.int32, (8 * ROWS, 128), 1)
    weights = cb[...].astype(F32)
    for j in range(2):
        own = slice(j * units, (j + 1) * units)
        mark = e * 2 + j
        scale = jnp.sum(
            jnp.where((wide == mark) | (wide == mark + 16), weights, 0.0), axis=1, keepdims=True
        )
        g, u, b = gacc[:, own], uacc[:, own], bacc[:, own] * scale
        s = jax.nn.sigmoid(g)
        act = g * s
        H[:, own] = (act * u * scale).astype(BF16)
        G[:, own] = (b * u * s * (1.0 + g * (1.0 - s))).astype(BF16)
        G[:, (2 + j) * units : (3 + j) * units] = (b * act).astype(BF16)

    def out_chunk(hh):
        for n in range(cols // 256):
            at = slice(n * 256, (n + 1) * 256)
            PO[hh, :, at] = jnp.dot(H[...], wd[hh, :, at], preferred_element_type=F32).astype(BF16)

    def grad_chunk(hh):
        for n in range(cols // 256):
            at = pl.ds(pl.multiple_of(hh * cols + n * 256, 256), 256)
            total = dot_nt(G[:, :units], wg[0, at, :])
            total += dot_nt(G[:, units : 2 * units], wg[1, at, :])
            total += dot_nt(G[:, 2 * units : 3 * units], wu[0, at, :])
            total += dot_nt(G[:, 3 * units :], wu[1, at, :])
            PG[hh, :, n * 256 : (n + 1) * 256] = total.astype(BF16)

    def to(i):
        return (z + i) % 4

    def add(acc, yy, xx, zz, terms):
        at = (yy * 2 + c, rows(xx, zz), slice(None))
        total = acc[at].astype(F32)
        for term in terms:
            total = total + term.astype(F32)
        return at, total

    FAR = ORDER + (0,)

    def core_send(acc, rc, base, yo):
        yy = (y, yn)[yo]
        send(acc.at[yy * 2 + cn], rc.at[yy], base + yo, dev_s)

    out_chunk(yn * 2 + cn)
    core_send(PO, RcO, RO, 1)
    out_chunk(yn * 2 + c)
    grad_chunk(yn * 2 + cn)
    core_send(PG, RcG, RG, 1)
    arrive(RcO.at[yn], RO + 1, dev_s)
    for a in (1, 0):
        for i in FAR:
            xx, zz = (x, xn)[a], to(i)
            at, total = add(PO, yn, xx, zz, [RcO[yn, rows(xx, zz), :]])
            PO[at] = total.astype(BF16)
            send(PO.at[at], RyO.at[rows(xx, zz), :], RO + 2 + 4 * a + i, dev_y)
    grad_chunk(yn * 2 + c)
    arrive(RcG.at[yn], RG + 1, dev_s)
    for i in FAR:
        at, total = add(PG, yn, xn, to(i), [RcG[yn, rows(xn, to(i)), :]])
        PG[at] = total.astype(BF16)
        send(PG.at[at], RxG.at[yn, half(to(i)), :], RG + 6 + i, dev_x)
    grad_chunk(y * 2 + cn)
    core_send(PG, RcG, RG, 0)
    grad_chunk(y * 2 + c)
    out_chunk(y * 2 + cn)
    core_send(PO, RcO, RO, 0)
    arrive(RcG.at[y], RG, dev_s)
    for i in FAR:
        at, total = add(PG, y, xn, to(i), [RcG[y, rows(xn, to(i)), :]])
        PG[at] = total.astype(BF16)
        send(PG.at[at], RxG.at[y, half(to(i)), :], RG + 2 + i, dev_x)
    out_chunk(y * 2 + c)
    arrive(RcO.at[y], RO, dev_s)
    for i in FAR:
        zz = to(i)
        arrive(RyO.at[rows(xn, zz), :], RO + 6 + i, dev_y)
        at, total = add(PO, y, xn, zz, [RcO[y, rows(xn, zz), :], RyO[rows(xn, zz), :]])
        PO[at] = total.astype(BF16)
        send(PO.at[at], RxO.at[half(zz), :], RO + 10 + i, dev_x)
        arrive(RxG.at[yn, half(zz), :], RG + 6 + i, dev_x)
        at, total = add(PG, yn, x, zz, [RcG[yn, rows(x, zz), :], RxG[yn, half(zz), :]])
        PG[at] = total.astype(BF16)
        send(PG.at[at], RyG.at[half(zz), :], RG + 10 + i, dev_y)
    for i in FAR:
        zz = to(i)
        for acc, rc, base, d1, d2, one, two, rz, res in (
            (PO, RcO, RO, dev_y, dev_x, RyO.at[rows(x, zz), :], RxO.at[half(zz), :], RzO, out),
            (PG, RcG, RG, dev_x, dev_y, RxG.at[y, half(zz), :], RyG.at[half(zz), :], RzG, grad),
        ):
            arrive(one, base + 2 + i, d1)
            arrive(two, base + 10 + i, d2)
            at, total = add(acc, y, x, zz, [rc[y, rows(x, zz), :], one[...], two[...]])
            if i:
                acc[at] = total.astype(BF16)
                send(acc.at[at], rz.at[i - 1], base + 14 + i - 1, dev_z[i])
            else:
                for k in ORDER:
                    arrive(rz.at[k - 1], base + 14 + k - 1, dev_z[k])
                    total = total + rz[k - 1].astype(F32)
                res[...] = total.astype(BF16)
    for copy in started:
        copy.wait_send()


def fused(tokens, routes, combine, w_gate, w_up, w_down, cotangent):
    cols = tokens.shape[1]
    units = w_gate.shape[2]
    width = w_gate.shape[1]
    all_rows = 8 * ROWS
    vmem = pl.BlockSpec(memory_space=pltpu.VMEM)
    hbm = pl.BlockSpec(memory_space=pl.ANY)
    bf = lambda *shape: pltpu.VMEM(shape, BF16)
    fl = lambda *shape: pltpu.VMEM(shape, F32)
    flops = 2 * all_rows * 6 * 2 * units * width
    return pl.pallas_call(
        kernel,
        out_shape=(
            jax.ShapeDtypeStruct(tokens.shape, BF16),
            jax.ShapeDtypeStruct(tokens.shape, BF16),
        ),
        in_specs=[vmem] * 4 + [hbm] * 3,
        out_specs=(vmem, vmem),
        scratch_shapes=[
            bf(4, all_rows, cols), bf(4, all_rows, cols),
            bf(2, width, units), bf(2, width, units), bf(4, 2 * units, cols),
            bf(all_rows, 128),
            fl(all_rows, 2 * units), fl(all_rows, 2 * units), fl(all_rows, 2 * units),
            bf(all_rows, 2 * units), bf(all_rows, 4 * units),
            bf(4, all_rows, cols), bf(4, all_rows, cols),
            bf(2, all_rows, cols), bf(2, all_rows, cols),
            bf(all_rows, cols), bf(4 * ROWS, cols), bf(3, ROWS, cols),
            bf(2, 4 * ROWS, cols), bf(4 * ROWS, cols), bf(3, ROWS, cols),
            pltpu.SemaphoreType.DMA((COPIES,)),
            pltpu.SemaphoreType.DMA((COPIES,)),
            pltpu.SemaphoreType.DMA((10,)),
        ],
        compiler_params=pltpu.CompilerParams(
            collective_id=0, has_side_effects=True, vmem_limit_bytes=52 * 2**20
        ),
        cost_estimate=pl.CostEstimate(
            flops=flops, bytes_accessed=2 * 3 * 2 * units * width, transcendentals=0
        ),
    )(tokens, cotangent, routes, combine, w_gate, w_up, w_down)


def solution(mesh):
    small = mesh.shape["expert"] == 8 and mesh.shape["hidden"] == 4
    return jax.shard_map(
        fused if small else per_device,
        mesh=mesh,
        in_specs=SPECS,
        out_specs=(P("expert", "hidden"), P("expert", "hidden")),
        check_vma=False,
    )
```

```python
import jax
import jax.numpy as jnp
from jax import lax
from jax.experimental import pallas as pl
from jax.experimental.pallas import tpu as pltpu
from jax.sharding import PartitionSpec as P


def per_device(tokens, routes, combine, w_gate, w_up, w_down, cotangent):
    tok_rows = tokens.shape[0]
    top_count = routes.shape[1]
    local_experts = w_gate.shape[0]
    sources = lax.axis_size("expert")
    experts = local_experts * sources
    pair_count = tok_rows * top_count
    capacity = 2 * pair_count // experts
    flat_routes = routes.reshape(pair_count)
    onehot = (flat_routes[:, None] == jnp.arange(experts, dtype=jnp.int32)[None, :]).astype(
        jnp.int32
    )
    slot_rank = jnp.sum((jnp.cumsum(onehot, axis=0) - 1) * onehot, axis=1)
    target = flat_routes * capacity + slot_rank
    slot_table = (
        jnp.full((experts * capacity,), pair_count, jnp.int32)
        .at[target]
        .set(jnp.arange(pair_count, dtype=jnp.int32))
    )
    source_rows = slot_table // top_count

    def pack_rows(values):
        padded = jnp.concatenate([values, jnp.zeros((1, values.shape[1]), values.dtype)], axis=0)
        return padded[source_rows].reshape(experts, capacity, values.shape[1])

    def to_local(arrived):
        columns = arrived.shape[2]
        sectioned = arrived.reshape(sources, local_experts, capacity, columns).transpose(1, 0, 2, 3)
        return sectioned.reshape(local_experts, sources * capacity, columns)

    def to_global(leaving):
        columns = leaving.shape[2]
        sectioned = leaving.reshape(local_experts, sources, capacity, columns).transpose(1, 0, 2, 3)
        return sectioned.reshape(experts, capacity, columns)

    def unpack(returned):
        flattened = returned.reshape(experts * capacity, returned.shape[2])
        picked = (
            flattened[target].astype(jnp.float32).reshape(tok_rows, top_count, returned.shape[2])
        )
        return jnp.sum(picked * combine[:, :, None], axis=1).astype(jnp.bfloat16)

    full_tokens, full_grads = (
        lax.all_gather(tokens, "hidden", axis=1, tiled=True),
        lax.all_gather(cotangent, "hidden", axis=1, tiled=True),
    )
    arrived_x, arrived_dy = (
        lax.all_to_all(pack_rows(full_tokens), "expert", split_axis=0, concat_axis=0, tiled=True),
        lax.all_to_all(pack_rows(full_grads), "expert", split_axis=0, concat_axis=0, tiled=True),
    )
    arrived_x = to_local(arrived_x)
    arrived_dy = to_local(arrived_dy)
    gate_pre = jnp.einsum("erd,edf->erf", arrived_x, w_gate, preferred_element_type=jnp.float32)
    up_pre = jnp.einsum("erd,edf->erf", arrived_x, w_up, preferred_element_type=jnp.float32)
    back_hidden = jnp.einsum("erd,efd->erf", arrived_dy, w_down, preferred_element_type=jnp.float32)
    sigmoid_gate = jax.nn.sigmoid(gate_pre)
    activated = gate_pre * sigmoid_gate
    hidden_act = (activated * up_pre).astype(jnp.bfloat16)
    out_terms = jnp.einsum(
        "erf,efd->erd", hidden_act, w_down, preferred_element_type=jnp.float32
    ).astype(jnp.bfloat16)
    grad_gate = (
        back_hidden * up_pre * sigmoid_gate * (1.0 + gate_pre * (1.0 - sigmoid_gate))
    ).astype(jnp.bfloat16)
    grad_up = (back_hidden * activated).astype(jnp.bfloat16)
    out_share = (
        lax.psum_scatter(out_terms, "hidden", scatter_dimension=2, tiled=True)
        .astype(jnp.float32)
        .astype(jnp.bfloat16)
    )
    out_back = lax.all_to_all(
        to_global(out_share), "expert", split_axis=0, concat_axis=0, tiled=True
    )
    grad_terms = jnp.einsum("erf,edf->erd", grad_gate, w_gate, preferred_element_type=jnp.float32)
    grad_terms = grad_terms + jnp.einsum(
        "erf,edf->erd", grad_up, w_up, preferred_element_type=jnp.float32
    )
    grad_share = lax.psum_scatter(
        grad_terms.astype(jnp.bfloat16), "hidden", scatter_dimension=2, tiled=True
    )
    grad_back = lax.all_to_all(
        to_global(grad_share), "expert", split_axis=0, concat_axis=0, tiled=True
    )
    return (unpack(out_back), unpack(grad_back))


SPECS = (
    P("expert", "hidden"),
    P("expert", None),
    P("expert", None),
    P("expert", None, "hidden"),
    P("expert", None, "hidden"),
    P("expert", "hidden", None),
    P("expert", "hidden"),
)
MESH = pl.DeviceIdType.MESH
ROWS = 16
ORDER = (1, 3, 2)
F32 = jnp.float32
BF16 = jnp.bfloat16
GT, GC, GW, RO, RG = 0, 31, 62, 66, 83
COPIES = 100


def dot_nt(a, b):
    return lax.dot_general(a, b, (((1,), (1,)), ((), ())), preferred_element_type=F32)


def kernel(
    tok, cot, routes, comb, wg_hbm, wu_hbm, wd_hbm, out, grad,
    X, Y, wg, wu, wd, cb, gacc, uacc, bacc, H, G,
    PO, PG, RcO, RcG, R1O, R2O, RzO, R1G, R2G, RzG, ssem, rsem, lsem,
):
    e, h = lax.axis_index("expert"), lax.axis_index("hidden")
    z, x, y, c = e // 2, e % 2, h // 2, h % 2
    xn, yn, cn = 1 - x, 1 - y, 1 - c
    cols = tok.shape[1]
    units = wd_hbm.shape[1]
    dev_x, dev_y, dev_s = (z * 2 + xn, h), (e, yn * 2 + c), (e, y * 2 + cn)
    xf, yf = c * x + (1 - c) * xn, c * yn + (1 - c) * y
    xs, ys = c * xn + (1 - c) * x, c * y + (1 - c) * yn
    dev_1, dev_2 = (z * 2 + xf, yf * 2 + c), (z * 2 + xs, ys * 2 + c)
    dev_z = {i: (((z + i) % 4) * 2 + x, h) for i in ORDER}

    def rows(xx, zz):
        return pl.ds(pl.multiple_of((xx * 4 + zz) * ROWS, ROWS), ROWS)

    started = []

    def send(src, dst, k, dev):
        copy = pltpu.make_async_remote_copy(
            src_ref=src, dst_ref=dst, send_sem=ssem.at[k], recv_sem=rsem.at[k],
            device_id=dev, device_id_type=MESH,
        )
        copy.start()
        started.append(copy)

    def arrive(ref, k, dev):
        pltpu.make_async_remote_copy(
            src_ref=ref, dst_ref=ref, send_sem=ssem.at[k], recv_sem=rsem.at[k],
            device_id=dev, device_id_type=MESH,
        ).wait_recv()

    barrier = pltpu.get_barrier_semaphore()
    partners = [dev_x, dev_y, dev_s] + [dev_z[i] for i in ORDER]
    for dev in partners:
        pl.semaphore_signal(barrier, inc=1, device_id=dev, device_id_type=MESH)

    X[h, rows(x, z), :] = tok[...]
    Y[h, rows(x, z), :] = cot[...]
    lane = lax.broadcasted_iota(jnp.int32, (ROWS, 128), 1)
    expert = jnp.where(lane < 16, lane, lane - 16)
    dense = jnp.zeros((ROWS, 128), F32)
    for k in range(routes.shape[1]):
        dense = dense + jnp.where(expert == routes[:, k : k + 1], comb[:, k : k + 1], 0.0)
    high = dense.astype(BF16)
    low = (dense - high.astype(F32)).astype(BF16)
    cb[rows(x, z), :] = jnp.where(lane < 16, high.astype(F32), low.astype(F32)).astype(BF16)
    pl.semaphore_wait(barrier, len(partners))

    def near(i):
        return (z - i) % 4

    def blk(buf, yy, cc, xx, i):
        return buf.at[yy * 2 + cc, rows(xx, near(i)), :]

    KINDS = ((y, x), (yf, xf), (ys, xs), (yn, xn))
    SIBS = ((y, x), (ys, xs), (yf, xf), (yn, xn))
    TOKS, COTS = (X, GT), (Y, GC)
    ALL = (0,) + ORDER

    def sib(arr, kind, i):
        ref = blk(arr[0], KINDS[kind][0], c, KINDS[kind][1], i)
        send(ref, ref, arr[1] + 15 + 4 * kind + i, dev_s)

    def sib_all(arr):
        for kind in range(4):
            for i in range(4):
                ref = blk(arr[0], SIBS[kind][0], cn, SIBS[kind][1], i)
                arrive(ref, arr[1] + 15 + 4 * kind + i, dev_s)

    def z_send(arr, i):
        ref = blk(arr[0], y, c, x, 0)
        send(ref, ref, arr[1] + i - 1, dev_z[i])

    def spread(arr, i):
        ref = blk(arr[0], y, c, x, i)
        if i:
            arrive(ref, arr[1] + i - 1, dev_z[i])
        send(ref, ref, arr[1] + 7 + i, dev_2)
        send(ref, ref, arr[1] + 3 + i, dev_1)
        sib(arr, 0, i)

    def from_first(arr, i):
        ref = blk(arr[0], yf, c, xf, i)
        arrive(ref, arr[1] + 3 + i, dev_1)
        send(ref, ref, arr[1] + 11 + i, dev_2)
        sib(arr, 1, i)

    def from_second(arr, a, i):
        ref = blk(arr[0], (ys, yn)[a], c, (xs, xn)[a], i)
        arrive(ref, arr[1] + 7 + 4 * a + i, dev_2)
        sib(arr, 2 + a, i)

    for i in ORDER:
        z_send(TOKS, i)
        if i == ORDER[0]:
            spread(TOKS, 0)
    for i in ORDER:
        ref = cb.at[rows(x, z), :]
        send(ref, ref, GW + i - 1, dev_z[i])
    for i in ORDER:
        z_send(COTS, i)

    wcopies = [
        pltpu.make_async_copy(wg_hbm, wg, lsem.at[0]),
        pltpu.make_async_copy(wu_hbm, wu, lsem.at[1]),
    ]
    for hh in range(4):
        for j in range(2):
            wcopies.append(
                pltpu.make_async_copy(
                    wd_hbm.at[j, :, pl.ds(hh * cols, cols)],
                    wd.at[hh, pl.ds(j * units, units), :],
                    lsem.at[2 + hh * 2 + j],
                )
            )
    for copy in wcopies:
        copy.start()

    gacc[...] = jnp.zeros_like(gacc)
    uacc[...] = jnp.zeros_like(uacc)
    bacc[...] = jnp.zeros_like(bacc)
    for i in ORDER:
        spread(TOKS, i)
    for i in ALL:
        from_first(TOKS, i)
    spread(COTS, 0)
    for i in ORDER:
        arrive(cb.at[rows(x, near(i)), :], GW + i - 1, dev_z[i])
    mine = cb.at[pl.ds(pl.multiple_of(x * 64, 64), 64), :]
    send(mine, mine, GW + 3, dev_x)
    for i in ALL:
        if i:
            spread(COTS, i)
        from_second(TOKS, 0, i)
    for i in ALL:
        from_second(TOKS, 1, i)

    def project(hh, _):
        at = pl.ds(pl.multiple_of(hh * cols, cols), cols)
        for j in range(2):
            own = slice(j * units, (j + 1) * units)
            gacc[:, own] += jnp.dot(X[hh], wg[j, at, :], preferred_element_type=F32)
            uacc[:, own] += jnp.dot(X[hh], wu[j, at, :], preferred_element_type=F32)
        return 0

    wcopies[0].wait()
    wcopies[1].wait()
    sib_all(TOKS)
    lax.fori_loop(0, 2, project, 0)
    for i in ALL:
        from_first(COTS, i)
    lax.fori_loop(2, 4, project, 0)

    other = cb.at[pl.ds(pl.multiple_of(xn * 64, 64), 64), :]
    arrive(other, GW + 3, dev_x)
    wide = lax.broadcasted_iota(jnp.int32, (8 * ROWS, 128), 1)
    weights = cb[...].astype(F32)
    scales = []
    for j in range(2):
        own = slice(j * units, (j + 1) * units)
        mark = e * 2 + j
        scale = jnp.sum(
            jnp.where((wide == mark) | (wide == mark + 16), weights, 0.0), axis=1, keepdims=True
        )
        scales.append(scale)
        g, u = gacc[:, own], uacc[:, own]
        H[:, own] = (g * jax.nn.sigmoid(g) * u * scale).astype(BF16)
    for copy in wcopies[2:]:
        copy.wait()

    def out_chunk(hh):
        for n in range(cols // 256):
            at = slice(n * 256, (n + 1) * 256)
            PO[hh, :, at] = jnp.dot(H[...], wd[hh, :, at], preferred_element_type=F32).astype(BF16)

    def grad_chunk(hh):
        for n in range(cols // 256):
            at = pl.ds(pl.multiple_of(hh * cols + n * 256, 256), 256)
            total = dot_nt(G[:, :units], wg[0, at, :])
            total += dot_nt(G[:, units : 2 * units], wg[1, at, :])
            total += dot_nt(G[:, 2 * units : 3 * units], wu[0, at, :])
            total += dot_nt(G[:, 3 * units :], wu[1, at, :])
            PG[hh, :, n * 256 : (n + 1) * 256] = total.astype(BF16)

    def to(i):
        return (z + i) % 4

    FAR = ORDER + (0,)
    OUTS, GRADS = (PO, RcO, R1O, R2O, RzO, RO, out), (PG, RcG, R1G, R2G, RzG, RG, grad)

    def core_send(res, yo):
        yy = (y, yn)[yo]
        send(res[0].at[yy * 2 + cn], res[1].at[yy], res[5] + yo, dev_s)

    def core_arrive(res, yo):
        arrive(res[1].at[(y, yn)[yo]], res[5] + yo, dev_s)

    def add(res, yy, xx, i, terms):
        at = (yy * 2 + c, rows(xx, to(i)), slice(None))
        total = res[0][at].astype(F32) + res[1][yy, rows(xx, to(i)), :].astype(F32)
        for term in terms:
            total = total + term.astype(F32)
        return at, total

    def first_sum(res, a):
        for i in FAR:
            at, total = add(res, (yn, yf)[a], (xn, xf)[a], i, [])
            res[0][at] = total.astype(BF16)
            send(res[0].at[at], res[2].at[a, i], res[5] + 2 + 4 * a + i, dev_1)

    def second_sum(res):
        for i in FAR:
            arrive(res[2].at[0, i], res[5] + 2 + i, dev_1)
            at, total = add(res, ys, xs, i, [res[2][0, i]])
            res[0][at] = total.astype(BF16)
            send(res[0].at[at], res[3].at[i], res[5] + 10 + i, dev_2)

    def z_total(res, i):
        arrive(res[2].at[1, i], res[5] + 6 + i, dev_1)
        arrive(res[3].at[i], res[5] + 10 + i, dev_2)
        return add(res, y, x, i, [res[2][1, i], res[3][i]])

    def z_sum(res):
        for i in ORDER:
            at, total = z_total(res, i)
            res[0][at] = total.astype(BF16)
            send(res[0].at[at], res[4].at[i - 1], res[5] + 14 + i - 1, dev_z[i])

    def last_sum(res):
        _, total = z_total(res, 0)
        for k in ORDER:
            arrive(res[4].at[k - 1], res[5] + 14 + k - 1, dev_z[k])
            total = total + res[4][k - 1].astype(F32)
        res[6][...] = total.astype(BF16)

    out_chunk(yn * 2 + cn)
    core_send(OUTS, 1)
    out_chunk(yn * 2 + c)
    out_chunk(y * 2 + cn)
    core_send(OUTS, 0)
    core_arrive(OUTS, 1)
    first_sum(OUTS, 0)
    out_chunk(y * 2 + c)
    core_arrive(OUTS, 0)
    first_sum(OUTS, 1)
    for a in range(2):
        for i in ALL:
            from_second(COTS, a, i)
    sib_all(COTS)

    def back(hh, _):
        bacc[...] += dot_nt(Y[hh], wd[hh])
        return 0

    lax.fori_loop(0, 4, back, 0)
    for j in range(2):
        own = slice(j * units, (j + 1) * units)
        g, u, b = gacc[:, own], uacc[:, own], bacc[:, own] * scales[j]
        s = jax.nn.sigmoid(g)
        G[:, own] = (b * u * s * (1.0 + g * (1.0 - s))).astype(BF16)
        G[:, (2 + j) * units : (3 + j) * units] = (b * g * s).astype(BF16)
    grad_chunk(yn * 2 + cn)
    core_send(GRADS, 1)
    second_sum(OUTS)
    grad_chunk(yn * 2 + c)
    core_arrive(GRADS, 1)
    first_sum(GRADS, 0)
    grad_chunk(y * 2 + cn)
    core_send(GRADS, 0)
    grad_chunk(y * 2 + c)
    core_arrive(GRADS, 0)
    first_sum(GRADS, 1)
    z_sum(OUTS)
    second_sum(GRADS)
    z_sum(GRADS)
    last_sum(OUTS)
    last_sum(GRADS)
    for copy in started:
        copy.wait_send()


def fused(tokens, routes, combine, w_gate, w_up, w_down, cotangent):
    cols = tokens.shape[1]
    units = w_gate.shape[2]
    width = w_gate.shape[1]
    all_rows = 8 * ROWS
    vmem = pl.BlockSpec(memory_space=pltpu.VMEM)
    hbm = pl.BlockSpec(memory_space=pl.ANY)
    bf = lambda *shape: pltpu.VMEM(shape, BF16)
    fl = lambda *shape: pltpu.VMEM(shape, F32)
    flops = 2 * all_rows * 6 * 2 * units * width
    return pl.pallas_call(
        kernel,
        out_shape=(
            jax.ShapeDtypeStruct(tokens.shape, BF16),
            jax.ShapeDtypeStruct(tokens.shape, BF16),
        ),
        in_specs=[vmem] * 4 + [hbm] * 3,
        out_specs=(vmem, vmem),
        scratch_shapes=[
            bf(4, all_rows, cols), bf(4, all_rows, cols),
            bf(2, width, units), bf(2, width, units), bf(4, 2 * units, cols),
            bf(all_rows, 128),
            fl(all_rows, 2 * units), fl(all_rows, 2 * units), fl(all_rows, 2 * units),
            bf(all_rows, 2 * units), bf(all_rows, 4 * units),
            bf(4, all_rows, cols), bf(4, all_rows, cols),
            bf(2, all_rows, cols), bf(2, all_rows, cols),
            bf(2, 4, ROWS, cols), bf(4, ROWS, cols), bf(3, ROWS, cols),
            bf(2, 4, ROWS, cols), bf(4, ROWS, cols), bf(3, ROWS, cols),
            pltpu.SemaphoreType.DMA((COPIES,)),
            pltpu.SemaphoreType.DMA((COPIES,)),
            pltpu.SemaphoreType.DMA((10,)),
        ],
        compiler_params=pltpu.CompilerParams(
            collective_id=0, has_side_effects=True, vmem_limit_bytes=52 * 2**20
        ),
        cost_estimate=pl.CostEstimate(
            flops=flops, bytes_accessed=2 * 3 * 2 * units * width, transcendentals=0
        ),
    )(tokens, cotangent, routes, combine, w_gate, w_up, w_down)


def solution(mesh):
    small = mesh.shape["expert"] == 8 and mesh.shape["hidden"] == 4
    return jax.shard_map(
        fused if small else per_device,
        mesh=mesh,
        in_specs=SPECS,
        out_specs=(P("expert", "hidden"), P("expert", "hidden")),
        check_vma=False,
    )
```

```python
import jax
import jax.numpy as jnp
from jax import lax
from jax.experimental import pallas as pl
from jax.experimental.pallas import tpu as pltpu
from jax.sharding import PartitionSpec as P


def per_device(tokens, routes, combine, w_gate, w_up, w_down, cotangent):
    tok_rows = tokens.shape[0]
    top_count = routes.shape[1]
    local_experts = w_gate.shape[0]
    sources = lax.axis_size("expert")
    experts = local_experts * sources
    pair_count = tok_rows * top_count
    capacity = 2 * pair_count // experts
    flat_routes = routes.reshape(pair_count)
    onehot = (flat_routes[:, None] == jnp.arange(experts, dtype=jnp.int32)[None, :]).astype(
        jnp.int32
    )
    slot_rank = jnp.sum((jnp.cumsum(onehot, axis=0) - 1) * onehot, axis=1)
    target = flat_routes * capacity + slot_rank
    slot_table = (
        jnp.full((experts * capacity,), pair_count, jnp.int32)
        .at[target]
        .set(jnp.arange(pair_count, dtype=jnp.int32))
    )
    source_rows = slot_table // top_count

    def pack_rows(values):
        padded = jnp.concatenate([values, jnp.zeros((1, values.shape[1]), values.dtype)], axis=0)
        return padded[source_rows].reshape(experts, capacity, values.shape[1])

    def to_local(arrived):
        columns = arrived.shape[2]
        sectioned = arrived.reshape(sources, local_experts, capacity, columns).transpose(1, 0, 2, 3)
        return sectioned.reshape(local_experts, sources * capacity, columns)

    def to_global(leaving):
        columns = leaving.shape[2]
        sectioned = leaving.reshape(local_experts, sources, capacity, columns).transpose(1, 0, 2, 3)
        return sectioned.reshape(experts, capacity, columns)

    def unpack(returned):
        flattened = returned.reshape(experts * capacity, returned.shape[2])
        picked = (
            flattened[target].astype(jnp.float32).reshape(tok_rows, top_count, returned.shape[2])
        )
        return jnp.sum(picked * combine[:, :, None], axis=1).astype(jnp.bfloat16)

    full_tokens, full_grads = (
        lax.all_gather(tokens, "hidden", axis=1, tiled=True),
        lax.all_gather(cotangent, "hidden", axis=1, tiled=True),
    )
    arrived_x, arrived_dy = (
        lax.all_to_all(pack_rows(full_tokens), "expert", split_axis=0, concat_axis=0, tiled=True),
        lax.all_to_all(pack_rows(full_grads), "expert", split_axis=0, concat_axis=0, tiled=True),
    )
    arrived_x = to_local(arrived_x)
    arrived_dy = to_local(arrived_dy)
    gate_pre = jnp.einsum("erd,edf->erf", arrived_x, w_gate, preferred_element_type=jnp.float32)
    up_pre = jnp.einsum("erd,edf->erf", arrived_x, w_up, preferred_element_type=jnp.float32)
    back_hidden = jnp.einsum("erd,efd->erf", arrived_dy, w_down, preferred_element_type=jnp.float32)
    sigmoid_gate = jax.nn.sigmoid(gate_pre)
    activated = gate_pre * sigmoid_gate
    hidden_act = (activated * up_pre).astype(jnp.bfloat16)
    out_terms = jnp.einsum(
        "erf,efd->erd", hidden_act, w_down, preferred_element_type=jnp.float32
    ).astype(jnp.bfloat16)
    grad_gate = (
        back_hidden * up_pre * sigmoid_gate * (1.0 + gate_pre * (1.0 - sigmoid_gate))
    ).astype(jnp.bfloat16)
    grad_up = (back_hidden * activated).astype(jnp.bfloat16)
    out_share = (
        lax.psum_scatter(out_terms, "hidden", scatter_dimension=2, tiled=True)
        .astype(jnp.float32)
        .astype(jnp.bfloat16)
    )
    out_back = lax.all_to_all(
        to_global(out_share), "expert", split_axis=0, concat_axis=0, tiled=True
    )
    grad_terms = jnp.einsum("erf,edf->erd", grad_gate, w_gate, preferred_element_type=jnp.float32)
    grad_terms = grad_terms + jnp.einsum(
        "erf,edf->erd", grad_up, w_up, preferred_element_type=jnp.float32
    )
    grad_share = lax.psum_scatter(
        grad_terms.astype(jnp.bfloat16), "hidden", scatter_dimension=2, tiled=True
    )
    grad_back = lax.all_to_all(
        to_global(grad_share), "expert", split_axis=0, concat_axis=0, tiled=True
    )
    return (unpack(out_back), unpack(grad_back))


SPECS = (
    P("expert", "hidden"),
    P("expert", None),
    P("expert", None),
    P("expert", None, "hidden"),
    P("expert", None, "hidden"),
    P("expert", "hidden", None),
    P("expert", "hidden"),
)
MESH = pl.DeviceIdType.MESH
ROWS = 16
ORDER = (1, 3, 2)
F32 = jnp.float32
BF16 = jnp.bfloat16
GT, GC, GW, RO, RG = 0, 31, 62, 66, 83
COPIES = 100


def dot_nt(a, b):
    return lax.dot_general(a, b, (((1,), (1,)), ((), ())), preferred_element_type=F32)


def kernel(
    tok_hbm, cot_hbm, routes_hbm, comb_hbm, wg_hbm, wu_hbm, wd_hbm, out, grad,
    X, Y, wg, wu, wd, cb, gacc, uacc, bacc, H, G,
    PO, PG, RcO, RcG, R1O, R2O, RzO, R1G, R2G, RzG, ssem, rsem, lsem, routes, comb,
):
    e, h = lax.axis_index("expert"), lax.axis_index("hidden")
    z, x, y, c = e // 2, e % 2, h // 2, h % 2
    xn, yn, cn = 1 - x, 1 - y, 1 - c
    cols = tok_hbm.shape[1]
    units = wd_hbm.shape[1]
    dev_x, dev_y, dev_s = (z * 2 + xn, h), (e, yn * 2 + c), (e, y * 2 + cn)
    xf, yf = c * x + (1 - c) * xn, c * yn + (1 - c) * y
    xs, ys = c * xn + (1 - c) * x, c * y + (1 - c) * yn
    dev_1, dev_2 = (z * 2 + xf, yf * 2 + c), (z * 2 + xs, ys * 2 + c)
    dev_z = {i: (((z + i) % 4) * 2 + x, h) for i in ORDER}

    def rows(xx, zz):
        return pl.ds(pl.multiple_of((xx * 4 + zz) * ROWS, ROWS), ROWS)

    started = []

    def send(src, dst, k, dev):
        copy = pltpu.make_async_remote_copy(
            src_ref=src, dst_ref=dst, send_sem=ssem.at[k], recv_sem=rsem.at[k],
            device_id=dev, device_id_type=MESH,
        )
        copy.start()
        started.append(copy)

    def arrive(ref, k, dev):
        pltpu.make_async_remote_copy(
            src_ref=ref, dst_ref=ref, send_sem=ssem.at[k], recv_sem=rsem.at[k],
            device_id=dev, device_id_type=MESH,
        ).wait_recv()

    barrier = pltpu.get_barrier_semaphore()
    partners = [dev_x, dev_y, dev_s] + [dev_z[i] for i in ORDER]
    for dev in partners:
        pl.semaphore_signal(barrier, inc=1, device_id=dev, device_id_type=MESH)

    own_in = [
        pltpu.make_async_copy(routes_hbm, routes, lsem.at[10]),
        pltpu.make_async_copy(comb_hbm, comb, lsem.at[11]),
        pltpu.make_async_copy(tok_hbm, X.at[h, rows(x, z), :], lsem.at[12]),
        pltpu.make_async_copy(cot_hbm, Y.at[h, rows(x, z), :], lsem.at[13]),
    ]
    for copy in own_in:
        copy.start()
    own_in[0].wait()
    own_in[1].wait()
    line = lax.broadcasted_iota(jnp.int32, (128, ROWS), 0)
    expert = jnp.where(line < 16, line, line - 16)
    dense = jnp.zeros((128, ROWS), F32)
    for k in range(routes.shape[0]):
        dense = dense + jnp.where(expert == routes[k : k + 1, :], comb[k : k + 1, :], 0.0)
    high = dense.astype(BF16).astype(F32)
    pair = jnp.where(line < 16, high, dense - high).astype(BF16)
    unit = jnp.where(
        lax.broadcasted_iota(jnp.int32, (ROWS, ROWS), 0)
        == lax.broadcasted_iota(jnp.int32, (ROWS, ROWS), 1),
        1.0,
        0.0,
    ).astype(BF16)
    cb[rows(x, z), :] = dot_nt(unit, pair).astype(BF16)
    own_in[2].wait()
    own_in[3].wait()
    pl.semaphore_wait(barrier, len(partners))

    def near(i):
        return (z - i) % 4

    def blk(buf, yy, cc, xx, i):
        return buf.at[yy * 2 + cc, rows(xx, near(i)), :]

    by_x, by_y, both_off = (y, xn), (yn, x), (yn, xn)
    TOKS = (X, GT, ((y, x), by_x, by_y, both_off), dev_x, dev_y)
    COTS = (Y, GC, ((y, x), by_y, by_x, both_off), dev_y, dev_x)
    ALL = (0,) + ORDER

    def sib(arr, kind, i):
        ref = blk(arr[0], arr[2][kind][0], c, arr[2][kind][1], i)
        send(ref, ref, arr[1] + 15 + 4 * kind + i, dev_s)

    def sib_all(arr, kinds):
        for kind in kinds:
            for i in range(4):
                ref = blk(arr[0], arr[2][kind][0], cn, arr[2][kind][1], i)
                arrive(ref, arr[1] + 15 + 4 * kind + i, dev_s)

    def z_send(arr, i):
        ref = blk(arr[0], y, c, x, 0)
        send(ref, ref, arr[1] + i - 1, dev_z[i])

    def spread(arr, i):
        ref = blk(arr[0], y, c, x, i)
        if i:
            arrive(ref, arr[1] + i - 1, dev_z[i])
        send(ref, ref, arr[1] + 3 + i, arr[3])
        send(ref, ref, arr[1] + 7 + i, arr[4])
        sib(arr, 0, i)

    def from_first(arr, i):
        ref = blk(arr[0], arr[2][1][0], c, arr[2][1][1], i)
        arrive(ref, arr[1] + 3 + i, arr[3])
        send(ref, ref, arr[1] + 11 + i, arr[4])
        sib(arr, 1, i)

    def from_second(arr, a, i):
        ref = blk(arr[0], arr[2][2 + a][0], c, arr[2][2 + a][1], i)
        arrive(ref, arr[1] + 7 + 4 * a + i, arr[4])
        sib(arr, 2 + a, i)

    for i in ORDER:
        z_send(TOKS, i)
        if i == ORDER[0]:
            spread(TOKS, 0)
    for i in ORDER:
        ref = cb.at[rows(x, z), :]
        send(ref, ref, GW + i - 1, dev_z[i])
    for i in ORDER:
        z_send(COTS, i)

    wcopies = [
        pltpu.make_async_copy(wg_hbm, wg, lsem.at[0]),
        pltpu.make_async_copy(wu_hbm, wu, lsem.at[1]),
    ]
    for hh in range(4):
        for j in range(2):
            wcopies.append(
                pltpu.make_async_copy(
                    wd_hbm.at[j, :, pl.ds(hh * cols, cols)],
                    wd.at[hh, pl.ds(j * units, units), :],
                    lsem.at[2 + hh * 2 + j],
                )
            )
    for copy in wcopies:
        copy.start()

    gacc[...] = jnp.zeros_like(gacc)
    uacc[...] = jnp.zeros_like(uacc)
    bacc[...] = jnp.zeros_like(bacc)
    for i in ORDER:
        spread(TOKS, i)
    spread(COTS, 0)
    for i in ALL:
        from_first(TOKS, i)

    def project(hh):
        at = pl.ds(pl.multiple_of(hh * cols, cols), cols)
        for j in range(2):
            own = slice(j * units, (j + 1) * units)
            gacc[:, own] += jnp.dot(X[hh], wg[j, at, :], preferred_element_type=F32)
            uacc[:, own] += jnp.dot(X[hh], wu[j, at, :], preferred_element_type=F32)

    wcopies[0].wait()
    wcopies[1].wait()
    project(y * 2 + c)
    for i in ORDER:
        arrive(cb.at[rows(x, near(i)), :], GW + i - 1, dev_z[i])
    mine = cb.at[pl.ds(pl.multiple_of(x * 64, 64), 64), :]
    send(mine, mine, GW + 3, dev_x)
    for i in ORDER:
        spread(COTS, i)
    for i in ALL:
        from_second(TOKS, 0, i)
    sib_all(TOKS, (0, 1))
    project(y * 2 + cn)
    for i in ALL:
        from_first(COTS, i)
        from_second(TOKS, 1, i)
    project(yn * 2 + c)
    for i in ALL:
        from_second(COTS, 0, i)
    sib_all(TOKS, (2, 3))
    project(yn * 2 + cn)

    other = cb.at[pl.ds(pl.multiple_of(xn * 64, 64), 64), :]
    arrive(other, GW + 3, dev_x)
    wide = lax.broadcasted_iota(jnp.int32, (8 * ROWS, 128), 1)
    weights = cb[...].astype(F32)
    scales = []
    for j in range(2):
        own = slice(j * units, (j + 1) * units)
        mark = e * 2 + j
        scale = jnp.sum(
            jnp.where((wide == mark) | (wide == mark + 16), weights, 0.0), axis=1, keepdims=True
        )
        scales.append(scale)
        g, u = gacc[:, own], uacc[:, own]
        H[:, own] = (g * jax.nn.sigmoid(g) * u * scale).astype(BF16)
    for copy in wcopies[2:]:
        copy.wait()

    def out_chunk(hh):
        for n in range(cols // 256):
            at = slice(n * 256, (n + 1) * 256)
            PO[hh, :, at] = jnp.dot(H[...], wd[hh, :, at], preferred_element_type=F32).astype(BF16)

    def grad_chunk(hh):
        for n in range(cols // 256):
            at = pl.ds(pl.multiple_of(hh * cols + n * 256, 256), 256)
            total = dot_nt(G[:, :units], wg[0, at, :])
            total += dot_nt(G[:, units : 2 * units], wg[1, at, :])
            total += dot_nt(G[:, 2 * units : 3 * units], wu[0, at, :])
            total += dot_nt(G[:, 3 * units :], wu[1, at, :])
            PG[hh, :, n * 256 : (n + 1) * 256] = total.astype(BF16)

    def to(i):
        return (z + i) % 4

    FAR = ORDER + (0,)
    OUTS, GRADS = (PO, RcO, R1O, R2O, RzO, RO, out), (PG, RcG, R1G, R2G, RzG, RG, grad)

    def core_send(res, yo):
        yy = (y, yn)[yo]
        send(res[0].at[yy * 2 + cn], res[1].at[yy], res[5] + yo, dev_s)

    def core_arrive(res, yo):
        arrive(res[1].at[(y, yn)[yo]], res[5] + yo, dev_s)

    def add(res, yy, xx, i, terms):
        at = (yy * 2 + c, rows(xx, to(i)), slice(None))
        total = res[0][at].astype(F32) + res[1][yy, rows(xx, to(i)), :].astype(F32)
        for term in terms:
            total = total + term.astype(F32)
        return at, total

    def first_sum(res, a):
        for i in FAR:
            at, total = add(res, (yn, yf)[a], (xn, xf)[a], i, [])
            res[0][at] = total.astype(BF16)
            send(res[0].at[at], res[2].at[a, i], res[5] + 2 + 4 * a + i, dev_1)

    def second_sum(res):
        for i in FAR:
            arrive(res[2].at[0, i], res[5] + 2 + i, dev_1)
            at, total = add(res, ys, xs, i, [res[2][0, i]])
            res[0][at] = total.astype(BF16)
            send(res[0].at[at], res[3].at[i], res[5] + 10 + i, dev_2)

    def z_total(res, i):
        arrive(res[2].at[1, i], res[5] + 6 + i, dev_1)
        arrive(res[3].at[i], res[5] + 10 + i, dev_2)
        return add(res, y, x, i, [res[2][1, i], res[3][i]])

    def z_sum(res):
        for i in ORDER:
            at, total = z_total(res, i)
            res[0][at] = total.astype(BF16)
            send(res[0].at[at], res[4].at[i - 1], res[5] + 14 + i - 1, dev_z[i])

    def last_sum(res):
        _, total = z_total(res, 0)
        for k in ORDER:
            arrive(res[4].at[k - 1], res[5] + 14 + k - 1, dev_z[k])
            total = total + res[4][k - 1].astype(F32)
        res[6][...] = total.astype(BF16)

    out_chunk(yn * 2 + cn)
    core_send(OUTS, 1)
    out_chunk(yn * 2 + c)
    out_chunk(y * 2 + cn)
    core_send(OUTS, 0)
    core_arrive(OUTS, 1)
    first_sum(OUTS, 0)
    out_chunk(y * 2 + c)
    core_arrive(OUTS, 0)
    first_sum(OUTS, 1)
    for i in ALL:
        from_second(COTS, 1, i)
    sib_all(COTS, range(4))

    def back(hh, _):
        bacc[...] += dot_nt(Y[hh], wd[hh])
        return 0

    lax.fori_loop(0, 4, back, 0)
    for j in range(2):
        own = slice(j * units, (j + 1) * units)
        g, u, b = gacc[:, own], uacc[:, own], bacc[:, own] * scales[j]
        s = jax.nn.sigmoid(g)
        G[:, own] = (b * u * s * (1.0 + g * (1.0 - s))).astype(BF16)
        G[:, (2 + j) * units : (3 + j) * units] = (b * g * s).astype(BF16)
    grad_chunk(yn * 2 + cn)
    core_send(GRADS, 1)
    second_sum(OUTS)
    grad_chunk(yn * 2 + c)
    core_arrive(GRADS, 1)
    first_sum(GRADS, 0)
    grad_chunk(y * 2 + cn)
    core_send(GRADS, 0)
    grad_chunk(y * 2 + c)
    core_arrive(GRADS, 0)
    first_sum(GRADS, 1)
    z_sum(OUTS)
    second_sum(GRADS)
    z_sum(GRADS)
    last_sum(OUTS)
    last_sum(GRADS)
    for copy in started:
        copy.wait_send()


def fused(tokens, routes, combine, w_gate, w_up, w_down, cotangent):
    cols = tokens.shape[1]
    units = w_gate.shape[2]
    width = w_gate.shape[1]
    all_rows = 8 * ROWS
    vmem = pl.BlockSpec(memory_space=pltpu.VMEM)
    hbm = pl.BlockSpec(memory_space=pltpu.HBM)
    bf = lambda *shape: pltpu.VMEM(shape, BF16)
    fl = lambda *shape: pltpu.VMEM(shape, F32)
    flops = 2 * all_rows * 6 * 2 * units * width
    return pl.pallas_call(
        kernel,
        out_shape=(
            jax.ShapeDtypeStruct(tokens.shape, BF16),
            jax.ShapeDtypeStruct(tokens.shape, BF16),
        ),
        in_specs=[hbm] * 7,
        out_specs=(vmem, vmem),
        scratch_shapes=[
            bf(4, all_rows, cols), bf(4, all_rows, cols),
            bf(2, width, units), bf(2, width, units), bf(4, 2 * units, cols),
            bf(all_rows, 128),
            fl(all_rows, 2 * units), fl(all_rows, 2 * units), fl(all_rows, 2 * units),
            bf(all_rows, 2 * units), bf(all_rows, 4 * units),
            bf(4, all_rows, cols), bf(4, all_rows, cols),
            bf(2, all_rows, cols), bf(2, all_rows, cols),
            bf(2, 4, ROWS, cols), bf(4, ROWS, cols), bf(3, ROWS, cols),
            bf(2, 4, ROWS, cols), bf(4, ROWS, cols), bf(3, ROWS, cols),
            pltpu.SemaphoreType.DMA((COPIES,)),
            pltpu.SemaphoreType.DMA((COPIES,)),
            pltpu.SemaphoreType.DMA((14,)),
            pltpu.VMEM(routes.shape[::-1], jnp.int32),
            fl(*routes.shape[::-1]),
        ],
        compiler_params=pltpu.CompilerParams(
            collective_id=0, has_side_effects=True, vmem_limit_bytes=64 * 2**20
        ),
        cost_estimate=pl.CostEstimate(
            flops=flops, bytes_accessed=2 * 3 * 2 * units * width, transcendentals=0
        ),
    )(tokens, cotangent, routes.T, combine.T, w_gate, w_up, w_down)


def solution(mesh):
    small = mesh.shape["expert"] == 8 and mesh.shape["hidden"] == 4
    return jax.shard_map(
        fused if small else per_device,
        mesh=mesh,
        in_specs=SPECS,
        out_specs=(P("expert", "hidden"), P("expert", "hidden")),
        check_vma=False,
    )
```

```python
import jax
import jax.numpy as jnp
from jax import lax
from jax.experimental import pallas as pl
from jax.experimental.pallas import tpu as pltpu
from jax.sharding import PartitionSpec as P


def per_device(tokens, routes, combine, w_gate, w_up, w_down, cotangent):
    tok_rows = tokens.shape[0]
    top_count = routes.shape[1]
    local_experts = w_gate.shape[0]
    sources = lax.axis_size("expert")
    experts = local_experts * sources
    pair_count = tok_rows * top_count
    capacity = 2 * pair_count // experts
    flat_routes = routes.reshape(pair_count)
    onehot = (flat_routes[:, None] == jnp.arange(experts, dtype=jnp.int32)[None, :]).astype(
        jnp.int32
    )
    slot_rank = jnp.sum((jnp.cumsum(onehot, axis=0) - 1) * onehot, axis=1)
    target = flat_routes * capacity + slot_rank
    slot_table = (
        jnp.full((experts * capacity,), pair_count, jnp.int32)
        .at[target]
        .set(jnp.arange(pair_count, dtype=jnp.int32))
    )
    source_rows = slot_table // top_count

    def pack_rows(values):
        padded = jnp.concatenate([values, jnp.zeros((1, values.shape[1]), values.dtype)], axis=0)
        return padded[source_rows].reshape(experts, capacity, values.shape[1])

    def to_local(arrived):
        columns = arrived.shape[2]
        sectioned = arrived.reshape(sources, local_experts, capacity, columns).transpose(1, 0, 2, 3)
        return sectioned.reshape(local_experts, sources * capacity, columns)

    def to_global(leaving):
        columns = leaving.shape[2]
        sectioned = leaving.reshape(local_experts, sources, capacity, columns).transpose(1, 0, 2, 3)
        return sectioned.reshape(experts, capacity, columns)

    def unpack(returned):
        flattened = returned.reshape(experts * capacity, returned.shape[2])
        picked = (
            flattened[target].astype(jnp.float32).reshape(tok_rows, top_count, returned.shape[2])
        )
        return jnp.sum(picked * combine[:, :, None], axis=1).astype(jnp.bfloat16)

    full_tokens, full_grads = (
        lax.all_gather(tokens, "hidden", axis=1, tiled=True),
        lax.all_gather(cotangent, "hidden", axis=1, tiled=True),
    )
    arrived_x, arrived_dy = (
        lax.all_to_all(pack_rows(full_tokens), "expert", split_axis=0, concat_axis=0, tiled=True),
        lax.all_to_all(pack_rows(full_grads), "expert", split_axis=0, concat_axis=0, tiled=True),
    )
    arrived_x = to_local(arrived_x)
    arrived_dy = to_local(arrived_dy)
    gate_pre = jnp.einsum("erd,edf->erf", arrived_x, w_gate, preferred_element_type=jnp.float32)
    up_pre = jnp.einsum("erd,edf->erf", arrived_x, w_up, preferred_element_type=jnp.float32)
    back_hidden = jnp.einsum("erd,efd->erf", arrived_dy, w_down, preferred_element_type=jnp.float32)
    sigmoid_gate = jax.nn.sigmoid(gate_pre)
    activated = gate_pre * sigmoid_gate
    hidden_act = (activated * up_pre).astype(jnp.bfloat16)
    out_terms = jnp.einsum(
        "erf,efd->erd", hidden_act, w_down, preferred_element_type=jnp.float32
    ).astype(jnp.bfloat16)
    grad_gate = (
        back_hidden * up_pre * sigmoid_gate * (1.0 + gate_pre * (1.0 - sigmoid_gate))
    ).astype(jnp.bfloat16)
    grad_up = (back_hidden * activated).astype(jnp.bfloat16)
    out_share = (
        lax.psum_scatter(out_terms, "hidden", scatter_dimension=2, tiled=True)
        .astype(jnp.float32)
        .astype(jnp.bfloat16)
    )
    out_back = lax.all_to_all(
        to_global(out_share), "expert", split_axis=0, concat_axis=0, tiled=True
    )
    grad_terms = jnp.einsum("erf,edf->erd", grad_gate, w_gate, preferred_element_type=jnp.float32)
    grad_terms = grad_terms + jnp.einsum(
        "erf,edf->erd", grad_up, w_up, preferred_element_type=jnp.float32
    )
    grad_share = lax.psum_scatter(
        grad_terms.astype(jnp.bfloat16), "hidden", scatter_dimension=2, tiled=True
    )
    grad_back = lax.all_to_all(
        to_global(grad_share), "expert", split_axis=0, concat_axis=0, tiled=True
    )
    return (unpack(out_back), unpack(grad_back))


SPECS = (
    P("expert", "hidden"),
    P("expert", None),
    P("expert", None),
    P("expert", None, "hidden"),
    P("expert", None, "hidden"),
    P("expert", "hidden", None),
    P("expert", "hidden"),
)
MESH = pl.DeviceIdType.MESH
ROWS = 16
ORDER = (1, 3, 2)
F32 = jnp.float32
BF16 = jnp.bfloat16
GT, GC, GW, RO, RG = 0, 31, 62, 66, 83
COPIES = 100


def dot_nt(a, b):
    return lax.dot_general(a, b, (((1,), (1,)), ((), ())), preferred_element_type=F32)


def kernel(
    tok_hbm, cot_hbm, routes_hbm, comb_hbm, wg_hbm, wu_hbm, wd_hbm, out, grad,
    X, Y, wg, wu, wd, cb, gacc, uacc, bacc, H, G,
    PO, PG, RcO, RcG, R1O, R2O, RzO, R1G, R2G, RzG, ssem, rsem, lsem, routes, comb,
):
    e, h = lax.axis_index("expert"), lax.axis_index("hidden")
    z, x, y, c = e // 2, e % 2, h // 2, h % 2
    xn, yn, cn = 1 - x, 1 - y, 1 - c
    cols = tok_hbm.shape[1]
    units = wd_hbm.shape[1]
    dev_x, dev_y, dev_s = (z * 2 + xn, h), (e, yn * 2 + c), (e, y * 2 + cn)
    xf, yf = c * x + (1 - c) * xn, c * yn + (1 - c) * y
    xs, ys = c * xn + (1 - c) * x, c * y + (1 - c) * yn
    dev_1, dev_2 = (z * 2 + xf, yf * 2 + c), (z * 2 + xs, ys * 2 + c)
    dev_z = {i: (((z + i) % 4) * 2 + x, h) for i in ORDER}

    def rows(xx, zz):
        return pl.ds(pl.multiple_of((xx * 4 + zz) * ROWS, ROWS), ROWS)

    started = []

    def send(src, dst, k, dev):
        copy = pltpu.make_async_remote_copy(
            src_ref=src, dst_ref=dst, send_sem=ssem.at[k], recv_sem=rsem.at[k],
            device_id=dev, device_id_type=MESH,
        )
        copy.start()
        started.append(copy)

    def arrive(ref, k, dev):
        pltpu.make_async_remote_copy(
            src_ref=ref, dst_ref=ref, send_sem=ssem.at[k], recv_sem=rsem.at[k],
            device_id=dev, device_id_type=MESH,
        ).wait_recv()

    barrier = pltpu.get_barrier_semaphore()
    partners = [dev_x, dev_y, dev_s] + [dev_z[i] for i in ORDER]
    for dev in partners:
        pl.semaphore_signal(barrier, inc=1, device_id=dev, device_id_type=MESH)

    own_in = [
        pltpu.make_async_copy(routes_hbm, routes, lsem.at[10]),
        pltpu.make_async_copy(comb_hbm, comb, lsem.at[11]),
        pltpu.make_async_copy(tok_hbm, X.at[h, rows(x, z), :], lsem.at[12]),
        pltpu.make_async_copy(cot_hbm, Y.at[h, rows(x, z), :], lsem.at[13]),
    ]
    for copy in own_in:
        copy.start()
    own_in[0].wait()
    own_in[1].wait()
    line = lax.broadcasted_iota(jnp.int32, (128, ROWS), 0)
    expert = jnp.where(line < 16, line, line - 16)
    dense = jnp.zeros((128, ROWS), F32)
    for k in range(routes.shape[0]):
        dense = dense + jnp.where(expert == routes[k : k + 1, :], comb[k : k + 1, :], 0.0)
    high = dense.astype(BF16).astype(F32)
    pair = jnp.where(line < 16, high, dense - high).astype(BF16)
    unit = jnp.where(
        lax.broadcasted_iota(jnp.int32, (ROWS, ROWS), 0)
        == lax.broadcasted_iota(jnp.int32, (ROWS, ROWS), 1),
        1.0,
        0.0,
    ).astype(BF16)
    cb[rows(x, z), :] = dot_nt(unit, pair).astype(BF16)
    own_in[2].wait()
    own_in[3].wait()
    pl.semaphore_wait(barrier, len(partners))

    def near(i):
        return (z - i) % 4

    def blk(buf, yy, cc, xx, i):
        return buf.at[yy * 2 + cc, rows(xx, near(i)), :]

    KINDS = ((y, x), (yf, xf), (ys, xs), (yn, xn))
    SIBS = ((y, x), (ys, xs), (yf, xf), (yn, xn))
    TOKS, COTS = (X, GT), (Y, GC)
    ALL = (0,) + ORDER

    def sib(arr, kind, i):
        ref = blk(arr[0], KINDS[kind][0], c, KINDS[kind][1], i)
        send(ref, ref, arr[1] + 15 + 4 * kind + i, dev_s)

    def sib_all(arr):
        for kind in range(4):
            for i in range(4):
                ref = blk(arr[0], SIBS[kind][0], cn, SIBS[kind][1], i)
                arrive(ref, arr[1] + 15 + 4 * kind + i, dev_s)

    def z_send(arr, i):
        ref = blk(arr[0], y, c, x, 0)
        send(ref, ref, arr[1] + i - 1, dev_z[i])

    def spread(arr, i):
        ref = blk(arr[0], y, c, x, i)
        if i:
            arrive(ref, arr[1] + i - 1, dev_z[i])
        send(ref, ref, arr[1] + 7 + i, dev_2)
        send(ref, ref, arr[1] + 3 + i, dev_1)
        sib(arr, 0, i)

    def from_first(arr, i):
        ref = blk(arr[0], yf, c, xf, i)
        arrive(ref, arr[1] + 3 + i, dev_1)
        send(ref, ref, arr[1] + 11 + i, dev_2)
        sib(arr, 1, i)

    def from_second(arr, a, i):
        ref = blk(arr[0], (ys, yn)[a], c, (xs, xn)[a], i)
        arrive(ref, arr[1] + 7 + 4 * a + i, dev_2)
        sib(arr, 2 + a, i)

    for i in ORDER:
        z_send(TOKS, i)
        if i == ORDER[0]:
            spread(TOKS, 0)
    for i in ORDER:
        ref = cb.at[rows(x, z), :]
        send(ref, ref, GW + i - 1, dev_z[i])
    for i in ORDER:
        z_send(COTS, i)

    wcopies = [
        pltpu.make_async_copy(wg_hbm, wg, lsem.at[0]),
        pltpu.make_async_copy(wu_hbm, wu, lsem.at[1]),
    ]
    for hh in range(4):
        for j in range(2):
            wcopies.append(
                pltpu.make_async_copy(
                    wd_hbm.at[j, :, pl.ds(hh * cols, cols)],
                    wd.at[hh, pl.ds(j * units, units), :],
                    lsem.at[2 + hh * 2 + j],
                )
            )
    for copy in wcopies:
        copy.start()

    gacc[...] = jnp.zeros_like(gacc)
    uacc[...] = jnp.zeros_like(uacc)
    bacc[...] = jnp.zeros_like(bacc)
    for i in ORDER:
        spread(TOKS, i)
    for i in ALL:
        from_first(TOKS, i)
    spread(COTS, 0)
    for i in ORDER:
        arrive(cb.at[rows(x, near(i)), :], GW + i - 1, dev_z[i])
    mine = cb.at[pl.ds(pl.multiple_of(x * 64, 64), 64), :]
    send(mine, mine, GW + 3, dev_x)
    for i in ALL:
        if i:
            spread(COTS, i)
        from_second(TOKS, 0, i)
    for i in ALL:
        from_second(TOKS, 1, i)

    def project(hh, _):
        at = pl.ds(pl.multiple_of(hh * cols, cols), cols)
        for j in range(2):
            own = slice(j * units, (j + 1) * units)
            gacc[:, own] += jnp.dot(X[hh], wg[j, at, :], preferred_element_type=F32)
            uacc[:, own] += jnp.dot(X[hh], wu[j, at, :], preferred_element_type=F32)
        return 0

    wcopies[0].wait()
    wcopies[1].wait()
    sib_all(TOKS)
    lax.fori_loop(0, 2, project, 0)
    for i in ALL:
        from_first(COTS, i)
    lax.fori_loop(2, 4, project, 0)

    other = cb.at[pl.ds(pl.multiple_of(xn * 64, 64), 64), :]
    arrive(other, GW + 3, dev_x)
    wide = lax.broadcasted_iota(jnp.int32, (8 * ROWS, 128), 1)
    weights = cb[...].astype(F32)
    scales = []
    for j in range(2):
        own = slice(j * units, (j + 1) * units)
        mark = e * 2 + j
        scale = jnp.sum(
            jnp.where((wide == mark) | (wide == mark + 16), weights, 0.0), axis=1, keepdims=True
        )
        scales.append(scale)
        g, u = gacc[:, own], uacc[:, own]
        H[:, own] = (g * jax.nn.sigmoid(g) * u * scale).astype(BF16)
    for copy in wcopies[2:]:
        copy.wait()

    def out_chunk(hh):
        for n in range(cols // 256):
            at = slice(n * 256, (n + 1) * 256)
            PO[hh, :, at] = jnp.dot(H[...], wd[hh, :, at], preferred_element_type=F32).astype(BF16)

    def grad_chunk(hh):
        for n in range(cols // 256):
            at = pl.ds(pl.multiple_of(hh * cols + n * 256, 256), 256)
            total = dot_nt(G[:, :units], wg[0, at, :])
            total += dot_nt(G[:, units : 2 * units], wg[1, at, :])
            total += dot_nt(G[:, 2 * units : 3 * units], wu[0, at, :])
            total += dot_nt(G[:, 3 * units :], wu[1, at, :])
            PG[hh, :, n * 256 : (n + 1) * 256] = total.astype(BF16)

    def to(i):
        return (z + i) % 4

    FAR = ORDER + (0,)
    OUTS, GRADS = (PO, RcO, R1O, R2O, RzO, RO, out), (PG, RcG, R1G, R2G, RzG, RG, grad)

    def core_send(res, yo):
        yy = (y, yn)[yo]
        send(res[0].at[yy * 2 + cn], res[1].at[yy], res[5] + yo, dev_s)

    def core_arrive(res, yo):
        arrive(res[1].at[(y, yn)[yo]], res[5] + yo, dev_s)

    def add(res, yy, xx, i, terms):
        at = (yy * 2 + c, rows(xx, to(i)), slice(None))
        total = res[0][at].astype(F32) + res[1][yy, rows(xx, to(i)), :].astype(F32)
        for term in terms:
            total = total + term.astype(F32)
        return at, total

    def first_sum(res, a):
        for i in FAR:
            at, total = add(res, (yn, yf)[a], (xn, xf)[a], i, [])
            res[0][at] = total.astype(BF16)
            send(res[0].at[at], res[2].at[a, i], res[5] + 2 + 4 * a + i, dev_1)

    def second_sum(res):
        for i in FAR:
            arrive(res[2].at[0, i], res[5] + 2 + i, dev_1)
            at, total = add(res, ys, xs, i, [res[2][0, i]])
            res[0][at] = total.astype(BF16)
            send(res[0].at[at], res[3].at[i], res[5] + 10 + i, dev_2)

    def z_total(res, i):
        arrive(res[2].at[1, i], res[5] + 6 + i, dev_1)
        arrive(res[3].at[i], res[5] + 10 + i, dev_2)
        return add(res, y, x, i, [res[2][1, i], res[3][i]])

    def z_sum(res):
        for i in ORDER:
            at, total = z_total(res, i)
            res[0][at] = total.astype(BF16)
            send(res[0].at[at], res[4].at[i - 1], res[5] + 14 + i - 1, dev_z[i])

    def last_sum(res):
        _, total = z_total(res, 0)
        for k in ORDER:
            arrive(res[4].at[k - 1], res[5] + 14 + k - 1, dev_z[k])
            total = total + res[4][k - 1].astype(F32)
        res[6][...] = total.astype(BF16)

    out_chunk(yn * 2 + cn)
    core_send(OUTS, 1)
    out_chunk(yn * 2 + c)
    out_chunk(y * 2 + cn)
    core_send(OUTS, 0)
    core_arrive(OUTS, 1)
    first_sum(OUTS, 0)
    out_chunk(y * 2 + c)
    core_arrive(OUTS, 0)
    first_sum(OUTS, 1)
    for a in range(2):
        for i in ALL:
            from_second(COTS, a, i)
    sib_all(COTS)

    def back(hh, _):
        bacc[...] += dot_nt(Y[hh], wd[hh])
        return 0

    lax.fori_loop(0, 4, back, 0)
    for j in range(2):
        own = slice(j * units, (j + 1) * units)
        g, u, b = gacc[:, own], uacc[:, own], bacc[:, own] * scales[j]
        s = jax.nn.sigmoid(g)
        G[:, own] = (b * u * s * (1.0 + g * (1.0 - s))).astype(BF16)
        G[:, (2 + j) * units : (3 + j) * units] = (b * g * s).astype(BF16)
    grad_chunk(yn * 2 + cn)
    core_send(GRADS, 1)
    second_sum(OUTS)
    grad_chunk(yn * 2 + c)
    core_arrive(GRADS, 1)
    first_sum(GRADS, 0)
    grad_chunk(y * 2 + cn)
    core_send(GRADS, 0)
    grad_chunk(y * 2 + c)
    core_arrive(GRADS, 0)
    first_sum(GRADS, 1)
    z_sum(OUTS)
    second_sum(GRADS)
    z_sum(GRADS)
    last_sum(OUTS)
    last_sum(GRADS)
    for copy in started:
        copy.wait_send()


def fused(tokens, routes, combine, w_gate, w_up, w_down, cotangent):
    cols = tokens.shape[1]
    units = w_gate.shape[2]
    width = w_gate.shape[1]
    all_rows = 8 * ROWS
    vmem = pl.BlockSpec(memory_space=pltpu.VMEM)
    hbm = pl.BlockSpec(memory_space=pltpu.HBM)
    bf = lambda *shape: pltpu.VMEM(shape, BF16)
    fl = lambda *shape: pltpu.VMEM(shape, F32)
    flops = 2 * all_rows * 6 * 2 * units * width
    return pl.pallas_call(
        kernel,
        out_shape=(
            jax.ShapeDtypeStruct(tokens.shape, BF16),
            jax.ShapeDtypeStruct(tokens.shape, BF16),
        ),
        in_specs=[hbm] * 7,
        out_specs=(vmem, vmem),
        scratch_shapes=[
            bf(4, all_rows, cols), bf(4, all_rows, cols),
            bf(2, width, units), bf(2, width, units), bf(4, 2 * units, cols),
            bf(all_rows, 128),
            fl(all_rows, 2 * units), fl(all_rows, 2 * units), fl(all_rows, 2 * units),
            bf(all_rows, 2 * units), bf(all_rows, 4 * units),
            bf(4, all_rows, cols), bf(4, all_rows, cols),
            bf(2, all_rows, cols), bf(2, all_rows, cols),
            bf(2, 4, ROWS, cols), bf(4, ROWS, cols), bf(3, ROWS, cols),
            bf(2, 4, ROWS, cols), bf(4, ROWS, cols), bf(3, ROWS, cols),
            pltpu.SemaphoreType.DMA((COPIES,)),
            pltpu.SemaphoreType.DMA((COPIES,)),
            pltpu.SemaphoreType.DMA((14,)),
            pltpu.VMEM(routes.shape[::-1], jnp.int32),
            fl(*routes.shape[::-1]),
        ],
        compiler_params=pltpu.CompilerParams(
            collective_id=0, has_side_effects=True, vmem_limit_bytes=52 * 2**20
        ),
        cost_estimate=pl.CostEstimate(
            flops=flops, bytes_accessed=2 * 3 * 2 * units * width, transcendentals=0
        ),
    )(tokens, cotangent, routes.T, combine.T, w_gate, w_up, w_down)


def solution(mesh):
    small = mesh.shape["expert"] == 8 and mesh.shape["hidden"] == 4
    return jax.shard_map(
        fused if small else per_device,
        mesh=mesh,
        in_specs=SPECS,
        out_specs=(P("expert", "hidden"), P("expert", "hidden")),
        check_vma=False,
    )
```
